512 devices in a mesh: gx: 8 (over y), gy: 8 (over z), gz: 8 (over x, core).
Axes of the slice: x: 4, y: 8, z: 8, core: 2. Of those that a mesh axis runs over, the one named last changes fastest.
Arguments:
- kinematics: float32 [18, 131072], P(None, ('gx', 'gy', 'gz')), may hold values from -6 to 6
- pair_offsets: float32 [3, 16, 131072], P(None, None, ('gx', 'gy', 'gz')), may hold values from -1 to 1
- pair_index: int32 [16, 131072], P(None, ('gx', 'gy', 'gz')), may hold values from 0 to 687, as said below
- neighbour_count: int32 [131072], P(('gx', 'gy', 'gz')), may hold values from 1 to 16
- send_rows: int32 [27, 8192], P(None, ('gx', 'gy', 'gz')), may hold values from 0 to 255
- migrate_dir: int32 [131072], P(('gx', 'gy', 'gz')), may hold values from 0 to 26, as said below
- migrate_slot: int32 [131072], P(('gx', 'gy', 'gz')), may hold values from 0 to 3, as said below
- enc_node_w1: float32 [15, 128], replicated, may hold values from -1.5 to 1.5
- enc_node_w2: bfloat16 [128, 128], replicated, may hold values from -0.5 to 0.5
- enc_edge_w1: float32 [4, 128], replicated, may hold values from -3 to 3
- enc_edge_w2: bfloat16 [128, 128], replicated, may hold values from -0.5 to 0.5
- edge_w1: bfloat16 [3, 384, 128], replicated, may hold values from -0.3125 to 0.3125
- edge_w2: bfloat16 [3, 128, 128], replicated, may hold values from -0.5 to 0.5
- node_w1: bfloat16 [3, 256, 128], replicated, may hold values from -0.375 to 0.375
- node_w2: bfloat16 [3, 128, 128], replicated, may hold values from -0.5 to 0.5
- edge_gain: float32 [3, 128], replicated, may hold values from 0.25 to 1.75
- node_gain: float32 [3, 128], replicated, may hold values from 0.25 to 1.75
- dec_w1: bfloat16 [128, 128], replicated, may hold values from -0.5 to 0.5
- dec_w2: float32 [3, 128], replicated, may hold values from -0.5 to 0.5
Outputs:
- stayed: float32 [18, 131072], P(None, ('gx', 'gy', 'gz'))
- arrived: float32 [18, 55296], P(None, ('gx', 'gy', 'gz'))
The draws below stay inside these ranges and needn't reach their ends.
Inputs may be any that keep to these rules, and one draw needn't show every extreme that they name: `pair_index`: A value below 256 names a row of the particle's own subdomain. A value v of 256 or more names ghost row v - 256; its direction (v - 256) // 16 is never 13 and points to a subdomain inside the grid. How many ghost rows of a direction are named differs between directions and subdomains. `migrate_dir`: A value other than 13 points to a subdomain inside the grid. On one subdomain at most 4 particles share a direction, and on every subdomain some direction has exactly 4. `migrate_slot`: among the particles of one subdomain that leave in one direction the slots are distinct; for staying particles the slot means nothing.
All inputs are finite; a program needn't handle non-finite values.
Results may differ from the reference program's by a relative error of at most 0.0085.
Values may be sent and summed in bfloat16 or wider, within the bound.
No kernel may reach another device: no remote copies, remote signals or barrier semaphores. Data moves between devices by JAX's collectives and lax.ppermute only.
A program may use at most 64 MiB of HBM per device.

```python
import jax
import jax.numpy as jnp
import numpy as np
from jax import lax

LATENT = 128
HIDDEN_SIZE = 128
PART_DEV = 256
K = 16
GHOST = 16
MIG = 4
ROUNDS = 3
STATE = 18
PARTICLES = 131072
SENDS = 8192
N_GX = 8
N_GY = 8
N_GZ = 8


def inside_table():
    device_total = N_GX * N_GY * N_GZ
    direction = np.arange(27)
    shifts = np.stack([direction // 9 - 1, direction // 3 % 3 - 1, direction % 3 - 1], axis=1)
    device = jnp.arange(device_total, dtype=jnp.int32)[:, None]
    along_first = device // (N_GY * N_GZ) + jnp.asarray(shifts[:, 0], jnp.int32)[None, :]
    along_second = device // N_GZ % N_GY + jnp.asarray(shifts[:, 1], jnp.int32)[None, :]
    along_third = device % N_GZ + jnp.asarray(shifts[:, 2], jnp.int32)[None, :]
    inside = (along_first >= 0) & (along_first < N_GX) & (along_second >= 0) & (along_second < N_GY) & (along_third >= 0) & (along_third < N_GZ)
    inside = inside & jnp.asarray(direction != 13)[None, :]
    kind_table = jnp.asarray(np.abs(shifts).sum(axis=1), jnp.int32)
    return (inside, kind_table)


def valid_order(inside):
    ranking = jnp.where(inside, 0, 1) * 32 + jnp.arange(27, dtype=jnp.int32)[None, :]
    ordered = jnp.argsort(ranking, axis=1).astype(jnp.int32)
    return (ordered, jnp.sum(inside.astype(jnp.int32), axis=1))


def draw_pair_index(key, part):
    device_total = N_GX * N_GY * N_GZ
    inside, kind_table = inside_table()
    ordered, valid_total = valid_order(inside)
    subkeys = jax.random.split(jax.random.fold_in(key, 11), 8)
    face_fill = jax.random.randint(subkeys[0], (device_total, 27), 3 * GHOST // 4, GHOST + 1)
    edge_fill = jax.random.randint(subkeys[1], (device_total, 27), GHOST // 2, GHOST + 1)
    corner_fill = jax.random.randint(subkeys[2], (device_total, 27), GHOST // 2, GHOST + 1)
    filled = jnp.where(kind_table[None, :] == 1, face_fill, jnp.where(kind_table[None, :] == 2, edge_fill, corner_fill))
    heavy_pick = jax.random.randint(subkeys[3], (device_total,), 0, valid_total)
    heavy_dir = jnp.take_along_axis(ordered, heavy_pick[:, None], axis=1)
    filled = jnp.where(jnp.arange(27, dtype=jnp.int32)[None, :] == heavy_dir, GHOST, filled)
    draw_shape = (K, device_total, PART_DEV)
    ghostly = jax.random.randint(subkeys[4], draw_shape, 0, 10) < 3
    local_row = jax.random.randint(subkeys[5], draw_shape, 0, PART_DEV)
    device = jnp.arange(device_total, dtype=jnp.int32)[None, :, None]
    picked_rank = jax.random.randint(subkeys[6], draw_shape, 0, valid_total[None, :, None])
    direction = ordered[device, picked_rank]
    slot_index = jax.random.randint(subkeys[7], draw_shape, 0, filled[device, direction])
    entries = jnp.where(ghostly, PART_DEV + direction * GHOST + slot_index, local_row)
    return entries.reshape(K, device_total * PART_DEV).astype(jnp.int32)


def migration_plan(key):
    device_total = N_GX * N_GY * N_GZ
    inside, kind_table = inside_table()
    ordered, valid_total = valid_order(inside)
    subkeys = jax.random.split(jax.random.fold_in(key, 23), 4)
    taken = jax.random.randint(subkeys[0], (device_total, 27), 0, MIG + 1)
    taken = jnp.where(inside, taken, 0)
    heavy_pick = jax.random.randint(subkeys[1], (device_total,), 0, valid_total)
    heavy_dir = jnp.take_along_axis(ordered, heavy_pick[:, None], axis=1)
    taken = jnp.where(jnp.arange(27, dtype=jnp.int32)[None, :] == heavy_dir, MIG, taken)
    permuted = jax.vmap(lambda subkey: jax.random.permutation(subkey, PART_DEV))(jax.random.split(subkeys[2], device_total))
    ranks = jnp.argsort(permuted, axis=1).astype(jnp.int32)
    direction = jnp.minimum(ranks // MIG, 26)
    slot_index = ranks % MIG
    device = jnp.arange(device_total, dtype=jnp.int32)[:, None]
    leaving = (ranks < 27 * MIG) & (slot_index < taken[device, direction])
    spare = jax.random.randint(subkeys[3], (device_total, PART_DEV), 0, MIG)
    targets = jnp.where(leaving, direction, 13)
    slots_out = jnp.where(leaving, slot_index, spare)
    return (targets.reshape(-1).astype(jnp.int32), slots_out.reshape(-1).astype(jnp.int32))


def draw_migrate_dir(key, part):
    return migration_plan(key)[0]


def draw_migrate_slot(key, part):
    return migration_plan(key)[1]


def plant(array, rng, low, top_value):
    spot = [jax.random.randint(jax.random.fold_in(rng, axis), (), 0, length) for axis, length in enumerate(array.shape)]
    main_axis = array.shape.index(max(array.shape))
    next_to = spot[:main_axis] + [(spot[main_axis] + 1) % array.shape[main_axis]] + spot[main_axis + 1:]
    return array.at[tuple(spot)].set(low).at[tuple(next_to)].set(top_value)


def level_of(key, extent, cuts, smallest, top_value):
    gain = 1.0
    for axis_at, blocks in cuts:
        draws = jax.random.uniform(jax.random.fold_in(jax.random.fold_in(key, 6), axis_at), (blocks,), jnp.float32, smallest / len(cuts), top_value / len(cuts))
        gain = gain * jnp.repeat(jnp.exp(draws), extent[axis_at] // blocks).reshape((-1,) + (1,) * (len(extent) - 1 - axis_at))
    return gain


def centred(stream_key, shape, deviation, reach, cuts=(), held_as=jnp.bfloat16):
    array = deviation * jax.random.normal(stream_key, shape, jnp.float32)
    if cuts:
        array = array * level_of(stream_key, shape, cuts, -0.22, 0.18)
    return jnp.clip(array, -reach, reach).astype(held_as)


def setup_inputs(seed: int = 0) -> dict:
    keys = jax.random.split(jax.random.key(seed), 20)
    return {
        "kinematics": centred(keys[0], (STATE, PARTICLES), 1.0, 6.0, ((1, 512),), jnp.float32),
        "pair_offsets": jnp.clip(jax.random.uniform(keys[1], (3, K, PARTICLES), jnp.float32, -1.0, 1.0) * level_of(keys[1], (3, K, PARTICLES), ((2, 512),), -0.4, 0.0), -1.0, 1.0),
        "pair_index": draw_pair_index(jax.random.fold_in(keys[19], 71), 0),
        "neighbour_count": plant(jax.random.randint(keys[3], (PARTICLES,), 1, K + 1), jax.random.fold_in(keys[3], 1), 1, K).astype(jnp.int32),
        "send_rows": plant(jax.random.randint(keys[4], (27, SENDS), 0, PART_DEV), jax.random.fold_in(keys[4], 1), 0, PART_DEV - 1).astype(jnp.int32),
        "migrate_dir": draw_migrate_dir(jax.random.fold_in(keys[19], 71), 0),
        "migrate_slot": draw_migrate_slot(jax.random.fold_in(keys[19], 71), 0),
        "enc_node_w1": centred(keys[7], (STATE - 3, HIDDEN_SIZE), (STATE - 3) ** -0.5, 1.5, (), jnp.float32),
        "enc_node_w2": centred(keys[8], (HIDDEN_SIZE, LATENT), HIDDEN_SIZE ** -0.5, 0.5),
        "enc_edge_w1": centred(keys[9], (4, HIDDEN_SIZE), 4 ** -0.5, 3.0, (), jnp.float32),
        "enc_edge_w2": centred(keys[10], (HIDDEN_SIZE, LATENT), HIDDEN_SIZE ** -0.5, 0.5),
        "edge_w1": centred(keys[11], (ROUNDS, 3 * LATENT, HIDDEN_SIZE), (3 * LATENT) ** -0.5, 0.3125),
        "edge_w2": centred(keys[12], (ROUNDS, HIDDEN_SIZE, LATENT), HIDDEN_SIZE ** -0.5, 0.5),
        "node_w1": centred(keys[13], (ROUNDS, 2 * LATENT, HIDDEN_SIZE), (2 * LATENT) ** -0.5, 0.375),
        "node_w2": centred(keys[14], (ROUNDS, HIDDEN_SIZE, LATENT), HIDDEN_SIZE ** -0.5, 0.5),
        "edge_gain": jnp.clip(1.0 + 0.15 * jax.random.normal(keys[15], (ROUNDS, LATENT), jnp.float32), 0.25, 1.75),
        "node_gain": jnp.clip(1.0 + 0.15 * jax.random.normal(keys[16], (ROUNDS, LATENT), jnp.float32), 0.25, 1.75),
        "dec_w1": centred(keys[17], (LATENT, HIDDEN_SIZE), LATENT ** -0.5, 0.5),
        "dec_w2": centred(keys[18], (3, HIDDEN_SIZE), HIDDEN_SIZE ** -0.5, 0.5, (), jnp.float32),
    }


norm_eps = 1e-05

def layer_norm(values):
    center = values - lax.optimization_barrier(jnp.mean(values, axis=-1, keepdims=True))
    spread = lax.optimization_barrier(jnp.mean(center * center, axis=-1, keepdims=True))
    return center * lax.rsqrt(spread + norm_eps)

def encode_edges(offsets, first_weight, second_weight):
    squared = lax.optimization_barrier(jnp.sum(offsets * offsets, axis=0, keepdims=True))
    features = jnp.concatenate([offsets, squared], axis=0)
    hidden = jnp.maximum(jnp.einsum('ckp,ch->kph', features, first_weight, precision=lax.Precision.HIGHEST), 0.0).astype(jnp.bfloat16)
    pair_slots, particles, inner_width = hidden.shape
    result = jnp.dot(hidden.reshape(pair_slots * particles, inner_width), second_weight, preferred_element_type=jnp.float32)
    return layer_norm(result).astype(jnp.bfloat16).reshape(pair_slots, particles, second_weight.shape[1])

def message_round(latent, extended, edge_latent, pair_index, neighbour_count, edge_first, edge_second, node_first, node_second, edge_scale, node_scale, block_pairs):
    latent_width = latent.shape[1]
    pair_slots, particles = pair_index.shape
    sender_proj = jnp.dot(extended, edge_first[2 * latent_width:], preferred_element_type=jnp.float32)
    receiver_proj = jnp.dot(latent, edge_first[latent_width:2 * latent_width], preferred_element_type=jnp.float32)
    summed = jnp.zeros((particles, edge_second.shape[1]), jnp.float32)
    for first_pair in range(0, pair_slots, block_pairs):
        chosen = pair_index[first_pair:first_pair + block_pairs]
        edge_rows = edge_latent[first_pair:first_pair + block_pairs].reshape(block_pairs * particles, latent_width)
        pre_act = jnp.dot(edge_rows, edge_first[:latent_width], preferred_element_type=jnp.float32).reshape(block_pairs, particles, -1)
        pre_act = pre_act + receiver_proj[None] + sender_proj[chosen]
        hidden = jnp.maximum(pre_act, 0.0).astype(jnp.bfloat16)
        message = layer_norm(jnp.dot(hidden.reshape(block_pairs * particles, -1), edge_second, preferred_element_type=jnp.float32)) * edge_scale
        message = message.reshape(block_pairs, particles, -1)
        usable = (first_pair + jnp.arange(block_pairs, dtype=jnp.int32))[:, None] < neighbour_count[None, :]
        summed = summed + lax.optimization_barrier(jnp.sum(jnp.where(usable[:, :, None], message, 0.0), axis=0))
    aggregate = summed.astype(jnp.bfloat16)
    node_pre = jnp.dot(latent, node_first[:latent_width], preferred_element_type=jnp.float32) + jnp.dot(aggregate, node_first[latent_width:], preferred_element_type=jnp.float32)
    node_mid = jnp.maximum(node_pre, 0.0).astype(jnp.bfloat16)
    update = layer_norm(jnp.dot(node_mid, node_second, preferred_element_type=jnp.float32)) * node_scale
    return (latent.astype(jnp.float32) + update).astype(jnp.bfloat16)

def direction_table():
    direction = np.arange(27)
    return np.stack([direction // 9 - 1, direction // 3 % 3 - 1, direction % 3 - 1], axis=1)

def neighbour_ids(device):
    shifts = jnp.asarray(direction_table(), dtype=jnp.int32)
    along_first = device // (N_GY * N_GZ) + shifts[:, 0]
    along_second = device // N_GZ % N_GY + shifts[:, 1]
    along_third = device % N_GZ + shifts[:, 2]
    inside = (along_first >= 0) & (along_first < N_GX) & (along_second >= 0) & (along_second < N_GY) & (along_third >= 0) & (along_third < N_GZ)
    other_id = (jnp.clip(along_first, 0, N_GX - 1) * N_GY + jnp.clip(along_second, 0, N_GY - 1)) * N_GZ + jnp.clip(along_third, 0, N_GZ - 1)
    return (other_id.astype(jnp.int32), inside)

def reference(kinematics, pair_offsets, pair_index, neighbour_count, send_rows, migrate_dir, migrate_slot, enc_node_w1, enc_node_w2, enc_edge_w1, enc_edge_w2, edge_w1, edge_w2, node_w1, node_w2, edge_gain, node_gain, dec_w1, dec_w2):
    device_total = N_GX * N_GY * N_GZ
    latent_width = enc_node_w2.shape[1]
    node_hidden = jnp.maximum(jnp.einsum('cn,ch->nh', kinematics[3:], enc_node_w1, precision=lax.Precision.HIGHEST), 0.0).astype(jnp.bfloat16)
    latent = layer_norm(jnp.dot(node_hidden, enc_node_w2, preferred_element_type=jnp.float32)).astype(jnp.bfloat16)
    latent = latent.reshape(device_total, PART_DEV, latent_width)
    offsets_split = pair_offsets.reshape(3, K, device_total, PART_DEV)
    pairs_split = pair_index.reshape(K, device_total, PART_DEV)
    counts_split = neighbour_count.reshape(device_total, PART_DEV)
    sends_split = send_rows.reshape(27, device_total, GHOST)
    backward = (26 - jnp.arange(27, dtype=jnp.int32)).astype(jnp.int32)
    for round_index in range(ROUNDS):

        def advance(device, latent=latent, round_index=round_index):
            other_id, inside = neighbour_ids(device)
            picked = sends_split[backward, other_id]
            ghosts = latent[other_id[:, None], picked]
            ghosts = jnp.where(inside[:, None, None], ghosts, jnp.zeros_like(ghosts))
            extended = jnp.concatenate([latent[device], ghosts.reshape(27 * GHOST, latent_width)], axis=0)
            edge_latent = encode_edges(offsets_split[:, :, device], enc_edge_w1, enc_edge_w2)
            return message_round(latent[device], extended, edge_latent, pairs_split[:, device], counts_split[device], edge_w1[round_index], edge_w2[round_index], node_w1[round_index], node_w2[round_index], edge_gain[round_index], node_gain[round_index], K)
        latent = lax.map(advance, jnp.arange(device_total, dtype=jnp.int32))
    flat_latent = latent.reshape(device_total * PART_DEV, latent_width)
    decode_hidden = jnp.maximum(jnp.dot(flat_latent, dec_w1, preferred_element_type=jnp.float32), 0.0).astype(jnp.bfloat16)
    acceleration = jnp.einsum('ch,nh->cn', dec_w2, decode_hidden.astype(jnp.float32), precision=lax.Precision.HIGHEST)
    velocity = kinematics[STATE - 3:] + acceleration
    new_state = jnp.concatenate([kinematics[:3] + velocity, kinematics[6:], velocity], axis=0)
    staying = migrate_dir == 13
    stayed = jnp.where(staying[None, :], new_state, 0.0)
    owner_device = (jnp.arange(device_total * PART_DEV, dtype=jnp.int32) // PART_DEV).astype(jnp.int32)
    target = jnp.where(staying, 27, migrate_dir).astype(jnp.int32)
    mailbox = jnp.zeros((device_total, 28, MIG, STATE), jnp.float32).at[owner_device, target, migrate_slot.astype(jnp.int32)].set(new_state.T)
    other_all, inside_all = jax.vmap(neighbour_ids)(jnp.arange(device_total, dtype=jnp.int32))
    received = mailbox[other_all, backward[None, :]]
    received = jnp.where(inside_all[:, :, None, None], received, 0.0)
    arrived = received.reshape(device_total * 27 * MIG, STATE).T
    return (stayed, arrived)
```

```python
import functools

import jax
import jax.numpy as jnp
from jax import lax
from jax.experimental import pallas as pl
from jax.experimental.pallas import tpu as pltpu
from jax.sharding import PartitionSpec as P

MIG = 4
EPS = 1e-05
F32 = jnp.float32
BF16 = jnp.bfloat16
VMEM_LIMIT = 48 * 1024 * 1024


def shifted(value, axis, steps):
    count = lax.axis_size(axis)
    first, last = (max(0, -steps), min(count, count - steps))
    return lax.ppermute(value, axis, [(source, source + steps) for source in range(first, last)])


def mm(a, b):
    return jnp.dot(a, b, preferred_element_type=F32)


def halves(value):
    high = value.astype(BF16)
    return high, (value - high.astype(F32)).astype(BF16)


def centred(weight):
    wide = weight.astype(F32)
    wide = wide - jnp.mean(wide, axis=-1, keepdims=True)
    return jnp.concatenate(halves(wide), axis=1)


def normalised(rows, weight):
    both = mm(rows, weight)
    width = both.shape[1] // 2
    center = both[:, :width] + both[:, width:]
    spread = jnp.mean(center * center, axis=-1, keepdims=True)
    return center, lax.rsqrt(spread + EPS)


def send_rows_of(latent, rows_ref, outs):
    particles = latent.shape[0]
    count = rows_ref.shape[0]
    picked = rows_ref[...] == lax.broadcasted_iota(jnp.int32, (count, particles), 1)
    chosen = mm(jnp.where(picked, 1.0, 0.0).astype(BF16), latent).astype(BF16)
    step = count // 3
    for index, out in enumerate(outs):
        out[...] = chosen[index * step : (index + 1) * step]


def node_kernel(kin_ref, w1_ref, w2_ref, rows_ref, latent_ref, low_ref, mid_ref, high_ref):
    features = kin_ref[3:, :]
    hidden = lax.dot_general(
        features,
        w1_ref[...],
        (((0,), (0,)), ((), ())),
        precision=lax.Precision.HIGHEST,
        preferred_element_type=F32,
    )
    hidden = jnp.maximum(hidden, 0.0).astype(BF16)
    center, scale = normalised(hidden, centred(w2_ref[...]))
    latent = (center * scale).astype(BF16)
    latent_ref[...] = latent
    send_rows_of(latent, rows_ref, (low_ref, mid_ref, high_ref))


def edge_kernel(off_ref, index_ref, count_ref, w1_ref, w2_ref, edge_ref, column_ref):
    slots, particles = index_ref.shape
    index = index_ref[...]
    place = index - particles
    slot = place & 15
    direction = place >> 4
    dx = (direction * 57) >> 9
    rest = direction - dx * 9
    dy = (rest * 11) >> 5
    dz = rest - dy * 3
    moved = particles + (dz * 9 + dx * 3 + dy) * 16 + slot
    index = jnp.where(index < particles, index, moved).astype(F32)
    count = count_ref[...].astype(F32)
    filler = jnp.zeros((128 - slots - count.shape[0], particles), F32)
    column_ref[...] = jnp.concatenate([index, count, filler], axis=0).T.astype(jnp.int32)

    offsets = [off_ref[c] for c in range(3)]
    square = offsets[0] * offsets[0] + offsets[1] * offsets[1] + offsets[2] * offsets[2]
    stack = jnp.concatenate(offsets + [square], axis=0)
    high = stack.astype(BF16).astype(F32)
    low = stack - high
    wide = jnp.concatenate([high, low, high, jnp.zeros_like(high)], axis=0).T.astype(BF16)
    first = w1_ref[...]
    width = first.shape[1]
    first_high = first.astype(BF16).astype(F32)
    first_low = first - first_high
    rows = [
        jnp.broadcast_to(part[c : c + 1], (slots, width))
        for part in (first_high, first_high, first_low, jnp.zeros_like(first))
        for c in range(4)
    ]
    table = jnp.concatenate(rows, axis=0)
    owner = lax.broadcasted_iota(jnp.int32, table.shape, 0) & (slots - 1)
    second = centred(w2_ref[...])
    for k in range(slots):
        chosen = jnp.where(owner == k, table, 0.0).astype(BF16)
        hidden = jnp.maximum(mm(wide, chosen), 0.0).astype(BF16)
        center, scale = normalised(hidden, second)
        edge_ref[k] = (center * scale).astype(BF16)


def updated_latent(
    round_index,
    slots,
    latent_ref,
    ghost_refs,
    edge_ref,
    column_ref,
    ew1_ref,
    ew2_ref,
    nw1_ref,
    nw2_ref,
    eg_ref,
    ng_ref,
):
    latent = latent_ref[...]
    particles, width = latent.shape
    total = particles + sum(ref.shape[0] for ref in ghost_refs)
    padded = -(-total // 256) * 256
    filler = jnp.zeros((padded - total, width), BF16)
    extended = jnp.concatenate([latent] + [ref[...] for ref in ghost_refs] + [filler], axis=0)
    receiver = mm(latent, ew1_ref[0, width : 2 * width])
    joint = jnp.concatenate([ew1_ref[0, :width], ew1_ref[0, 2 * width :]], axis=0)
    second = centred(ew2_ref[0])
    lanes = lax.broadcasted_iota(jnp.int32, (particles, padded), 1)
    counts = column_ref[:, slots : slots + 1]
    summed = jnp.zeros((particles, width), F32)
    for k in range(slots):
        picked = column_ref[:, k : k + 1] == lanes
        sender = mm(jnp.where(picked, 1.0, 0.0).astype(BF16), extended).astype(BF16)
        pre = mm(jnp.concatenate([edge_ref[k], sender], axis=1), joint) + receiver
        hidden = jnp.maximum(pre, 0.0).astype(BF16)
        center, scale = normalised(hidden, second)
        summed = summed + center * jnp.where(counts > k, scale, 0.0)
    aggregate = (summed * eg_ref[round_index : round_index + 1]).astype(BF16)
    node_pre = mm(jnp.concatenate([latent, aggregate], axis=1), nw1_ref[0])
    node_mid = jnp.maximum(node_pre, 0.0).astype(BF16)
    center, scale = normalised(node_mid, centred(nw2_ref[0]))
    update = center * scale * ng_ref[round_index : round_index + 1]
    return (latent.astype(F32) + update).astype(BF16)


def round_kernel(round_index, slots, latent_ref, g0, g1, g2, *refs):
    (edge, column, ew1, ew2, nw1, nw2, eg, ng, rows_ref, out_ref, low, mid, high) = refs
    latent = updated_latent(
        round_index, slots, latent_ref, (g0, g1, g2), edge, column, ew1, ew2, nw1, nw2, eg, ng
    )
    out_ref[...] = latent
    send_rows_of(latent, rows_ref, (low, mid, high))


def last_kernel(round_index, slots, latent_ref, g0, g1, g2, *refs):
    (edge, column, ew1, ew2, nw1, nw2, eg, ng) = refs[:8]
    (kin_ref, leave_ref, dw1_ref, dw2_ref, stayed_ref, low, mid, high) = refs[8:]
    latent = updated_latent(
        round_index, slots, latent_ref, (g0, g1, g2), edge, column, ew1, ew2, nw1, nw2, eg, ng
    )
    decoded = jnp.maximum(mm(latent, dw1_ref[...]), 0.0)
    decoded = decoded.astype(BF16).astype(F32)
    acceleration = lax.dot_general(
        dw2_ref[...],
        decoded,
        (((1,), (1,)), ((), ())),
        precision=lax.Precision.HIGHEST,
        preferred_element_type=F32,
    )
    state_rows, particles = kin_ref.shape
    velocity = kin_ref[state_rows - 3 :, :] + acceleration
    state = jnp.concatenate([kin_ref[:3, :] + velocity, kin_ref[6:, :], velocity], axis=0)
    direction = leave_ref[0:1, :]
    staying = direction == 13
    stayed_ref[...] = jnp.where(staying, state, 0.0)
    code = jnp.where(staying, -1, direction * MIG + leave_ref[1:2, :])
    picker = jnp.where(
        code == lax.broadcasted_iota(jnp.int32, (27 * MIG, particles), 0), 1.0, 0.0
    )
    outgoing = lax.dot_general(
        picker,
        state,
        (((1,), (1,)), ((), ())),
        precision=lax.Precision.HIGHEST,
        preferred_element_type=F32,
    )
    step = 9 * MIG
    for index, out in enumerate((low, mid, high)):
        out[...] = outgoing[index * step : (index + 1) * step]


def whole(shape):
    return pl.BlockSpec(shape, lambda i: (0,) * len(shape))


def call(body, args, specs, outs, name, flops=0, moved=0):
    return pl.pallas_call(
        body,
        grid=(1,),
        in_specs=[spec if spec is not None else whole(a.shape) for a, spec in zip(args, specs)],
        out_specs=[whole(s.shape) for s in outs],
        out_shape=outs,
        compiler_params=pltpu.CompilerParams(vmem_limit_bytes=VMEM_LIMIT),
        cost_estimate=pl.CostEstimate(flops=flops, bytes_accessed=moved, transcendentals=0),
        name=name,
    )(*args)


def shape(dims, dtype):
    return jax.ShapeDtypeStruct(dims, dtype)


def exchanged(low, mid, high, rows):
    tail = low.shape[-1]
    parts = [shifted(high, "gx", 1), mid, shifted(low, "gx", -1)]
    parts = [part.reshape(3, 3 * rows, tail) for part in parts]
    low, mid, high = (
        jnp.concatenate([part[y] for part in parts], axis=0) for y in range(3)
    )
    parts = [shifted(high, "gy", 1), mid, shifted(low, "gy", -1)]
    parts = [part.reshape(3, 3, rows, tail) for part in parts]
    low, mid, high = (
        jnp.stack([part[:, z] for part in parts], axis=1).reshape(9 * rows, tail)
        for z in range(3)
    )
    return [shifted(high, "gz", 1), mid, shifted(low, "gz", -1)]


def on_device(
    kinematics,
    pair_offsets,
    pair_index,
    neighbour_count,
    send_rows,
    migrate_dir,
    migrate_slot,
    enc_node_w1,
    enc_node_w2,
    enc_edge_w1,
    enc_edge_w2,
    edge_w1,
    edge_w2,
    node_w1,
    node_w2,
    edge_gain,
    node_gain,
    dec_w1,
    dec_w2,
):
    width = enc_node_w2.shape[1]
    slots, particles = pair_index.shape
    ghost_rows = send_rows.shape[1]
    rounds = edge_w1.shape[0]
    state_rows = kinematics.shape[0]
    rows = send_rows.reshape(-1, 1)
    part = shape((9 * ghost_rows, width), BF16)
    latent, low, mid, high = call(
        node_kernel,
        (kinematics, enc_node_w1, enc_node_w2, rows),
        (None,) * 4,
        [shape((particles, width), BF16), part, part, part],
        "node_encoder",
    )
    edges, columns = call(
        edge_kernel,
        (
            pair_offsets,
            pair_index,
            neighbour_count.reshape(1, particles),
            enc_edge_w1,
            enc_edge_w2,
        ),
        (None,) * 5,
        [shape((slots, particles, width), BF16), shape((particles, 128), jnp.int32)],
        "edge_encoder",
        flops=2 * slots * particles * 256 * 384,
        moved=4 * slots * particles * width,
    )
    leaving = jnp.stack([migrate_dir, migrate_slot], axis=0)
    for r in range(rounds):
        ghosts = exchanged(low, mid, high, ghost_rows)

        def of_round(array):
            return pl.BlockSpec((1,) + array.shape[1:], lambda i: (r, 0, 0))

        args = [latent, *ghosts, edges, columns, edge_w1, edge_w2, node_w1, node_w2]
        specs = [None] * 6 + [of_round(a) for a in args[6:]]
        args += [edge_gain, node_gain]
        specs += [None, None]
        if r < rounds - 1:
            latent, low, mid, high = call(
                functools.partial(round_kernel, r, slots),
                args + [rows],
                specs + [None],
                [shape((particles, width), BF16), part, part, part],
                "message_round",
            )
        else:
            out = shape((9 * MIG, state_rows), F32)
            stayed, low, mid, high = call(
                functools.partial(last_kernel, r, slots),
                args + [kinematics, leaving, dec_w1, dec_w2],
                specs + [None] * 4,
                [shape((state_rows, particles), F32), out, out, out],
                "last_round",
            )
    landed = exchanged(low, mid, high, MIG)
    landed = jnp.stack([g.reshape(9, MIG, state_rows) for g in landed], axis=1)
    arrived = landed.reshape(27 * MIG, state_rows).T
    return (stayed, arrived)


def solution(mesh):
    axes = ("gx", "gy", "gz")
    return jax.shard_map(
        on_device,
        mesh=mesh,
        in_specs=(
            P(None, axes),
            P(None, None, axes),
            P(None, axes),
            P(axes),
            P(None, axes),
            P(axes),
            P(axes),
        )
        + (P(),) * 12,
        out_specs=(P(None, axes), P(None, axes)),
        check_vma=False,
    )
```

```python
import functools

import jax
import jax.numpy as jnp
from jax import lax
from jax.experimental import pallas as pl
from jax.experimental.pallas import tpu as pltpu
from jax.sharding import PartitionSpec as P

MIG = 4
BLOCK = 8
EPS = 1e-05
F32 = jnp.float32
BF16 = jnp.bfloat16
VMEM_LIMIT = 48 * 1024 * 1024


def shifted(value, axis, steps):
    count = lax.axis_size(axis)
    first, last = (max(0, -steps), min(count, count - steps))
    return lax.ppermute(value, axis, [(source, source + steps) for source in range(first, last)])


def mm(a, b):
    return jnp.dot(a, b, preferred_element_type=F32)


def halves(value):
    high = value.astype(BF16)
    return high, (value - high.astype(F32)).astype(BF16)


def centred(weight):
    wide = weight.astype(F32)
    wide = wide - jnp.mean(wide, axis=-1, keepdims=True)
    return jnp.concatenate(halves(wide), axis=1)


def normalised(rows, weight):
    both = mm(rows, weight)
    width = both.shape[1] // 2
    center = both[:, :width] + both[:, width:]
    spread = jnp.mean(center * center, axis=-1, keepdims=True)
    return center, lax.rsqrt(spread + EPS)


def send_rows_of(latent, rows_ref, outs):
    particles = latent.shape[0]
    depth = rows_ref.shape[0]
    lanes = lax.broadcasted_iota(jnp.int32, (depth, particles), 1)
    for z, out in enumerate(outs):
        picked = [
            jnp.where(rows_ref[:, d : d + 1] == lanes, 1.0, 0.0)
            for d in [x * 9 + y * 3 + z for x in range(3) for y in range(3)]
        ]
        picked = jnp.concatenate(picked, axis=0).astype(BF16)
        out[...] = mm(picked, latent).astype(BF16)


def split_direction(direction):
    dx = (direction * 57) >> 9
    rest = direction - dx * 9
    dy = (rest * 11) >> 5
    return dx, dy, rest - dy * 3


def node_kernel(kin_ref, w1_ref, w2_ref, rows_ref, latent_ref, low_ref, mid_ref, high_ref):
    features = kin_ref[3:, :]
    hidden = lax.dot_general(
        features,
        w1_ref[...],
        (((0,), (0,)), ((), ())),
        precision=lax.Precision.HIGHEST,
        preferred_element_type=F32,
    )
    hidden = jnp.maximum(hidden, 0.0).astype(BF16)
    center, scale = normalised(hidden, centred(w2_ref[...]))
    latent = (center * scale).astype(BF16)
    latent_ref[...] = latent
    send_rows_of(latent, rows_ref, (low_ref, mid_ref, high_ref))


def edge_kernel(off_ref, index_ref, count_ref, w1_ref, w2_ref, edge_ref, column_ref):
    slots, particles = index_ref.shape
    index = index_ref[...]
    place = index - particles
    slot = place & 15
    dx, dy, dz = split_direction(place >> 4)
    moved = particles + (dy * 9 + dz * 3 + dx) * 16 + slot
    index = jnp.where(index < particles, index, moved).astype(F32)
    count = count_ref[...].astype(F32)
    filler = jnp.zeros((128 - slots - count.shape[0], particles), F32)
    column_ref[...] = jnp.concatenate([index, count, filler], axis=0).T.astype(jnp.int32)

    offsets = [off_ref[c] for c in range(3)]
    square = offsets[0] * offsets[0] + offsets[1] * offsets[1] + offsets[2] * offsets[2]
    stack = jnp.concatenate(offsets + [square], axis=0)
    high = stack.astype(BF16).astype(F32)
    low = stack - high
    wide = jnp.concatenate([high, low, high, jnp.zeros_like(high)], axis=0).T.astype(BF16)
    first = w1_ref[...]
    width = first.shape[1]
    first_high = first.astype(BF16).astype(F32)
    first_low = first - first_high
    rows = [
        jnp.broadcast_to(part[c : c + 1], (slots, width))
        for part in (first_high, first_high, first_low, jnp.zeros_like(first))
        for c in range(4)
    ]
    table = jnp.concatenate(rows, axis=0)
    owner = lax.broadcasted_iota(jnp.int32, table.shape, 0) & (slots - 1)
    second = centred(w2_ref[...])
    for k in range(slots):
        chosen = jnp.where(owner == k, table, 0.0).astype(BF16)
        hidden = jnp.maximum(mm(wide, chosen), 0.0).astype(BF16)
        center, scale = normalised(hidden, second)
        edge_ref[k] = (center * scale).astype(BF16)


def one_hot(column_ref, first, count, lanes):
    picked = [
        jnp.where(column_ref[:, k : k + 1] == lanes, 1.0, 0.0).astype(BF16)
        for k in range(first, first + count)
    ]
    return jnp.concatenate(picked, axis=0)


def local_kernel(latent_ref, edge_ref, column_ref, w1_ref, out_ref):
    slots, particles, width = edge_ref.shape
    latent = latent_ref[...]
    receiver = mm(latent, w1_ref[0, width : 2 * width])
    sender = jnp.concatenate(halves(mm(latent, w1_ref[0, 2 * width :])), axis=1)
    first = w1_ref[0, :width]
    lanes = lax.broadcasted_iota(jnp.int32, (particles, particles), 1)
    for k in range(0, slots, BLOCK):
        both = mm(one_hot(column_ref, k, BLOCK, lanes), sender)
        pre = mm(edge_ref[k : k + BLOCK].reshape(BLOCK * particles, width), first)
        pre = pre + both[:, :width] + both[:, width:]
        for j in range(BLOCK):
            out_ref[k + j] = pre[j * particles : (j + 1) * particles] + receiver


def updated_latent(r, latent_ref, ghost_refs, part_ref, column_ref, refs):
    ew1_ref, ew2_ref, nw1_ref, nw2_ref, eg_ref, ng_ref = refs
    latent = latent_ref[...]
    slots, particles, width = part_ref.shape
    total = sum(ref.shape[0] for ref in ghost_refs)
    padded = -(-total // 256) * 256
    filler = jnp.zeros((padded - total, width), BF16)
    ghosts = jnp.concatenate([ref[...] for ref in ghost_refs] + [filler], axis=0)
    sender = jnp.concatenate(halves(mm(ghosts, ew1_ref[0, 2 * width :])), axis=1)
    second = centred(ew2_ref[0])
    lanes = lax.broadcasted_iota(jnp.int32, (particles, padded), 1) + particles
    counts = column_ref[:, slots : slots + 1]
    summed = jnp.zeros((particles, width), F32)
    for k in range(0, slots, BLOCK):
        both = mm(one_hot(column_ref, k, BLOCK, lanes), sender)
        pre = part_ref[k : k + BLOCK].reshape(BLOCK * particles, width)
        pre = pre + both[:, :width] + both[:, width:]
        hidden = jnp.maximum(pre, 0.0).astype(BF16)
        center, scale = normalised(hidden, second)
        for j in range(BLOCK):
            rows = slice(j * particles, (j + 1) * particles)
            summed = summed + center[rows] * jnp.where(counts > k + j, scale[rows], 0.0)
    aggregate = (summed * eg_ref[r : r + 1]).astype(BF16)
    node_pre = mm(jnp.concatenate([latent, aggregate], axis=1), nw1_ref[0])
    node_mid = jnp.maximum(node_pre, 0.0).astype(BF16)
    center, scale = normalised(node_mid, centred(nw2_ref[0]))
    update = center * scale * ng_ref[r : r + 1]
    return (latent.astype(F32) + update).astype(BF16)


def round_kernel(r, latent_ref, g0, g1, g2, part_ref, column_ref, *refs):
    rows_ref, out_ref, low, mid, high = refs[6:]
    latent = updated_latent(r, latent_ref, (g0, g1, g2), part_ref, column_ref, refs[:6])
    out_ref[...] = latent
    send_rows_of(latent, rows_ref, (low, mid, high))


def last_kernel(r, latent_ref, g0, g1, g2, part_ref, column_ref, *refs):
    kin_ref, leave_ref, dw1_ref, dw2_ref, stayed_ref, low, mid, high = refs[6:]
    latent = updated_latent(r, latent_ref, (g0, g1, g2), part_ref, column_ref, refs[:6])
    decoded = jnp.maximum(mm(latent, dw1_ref[...]), 0.0)
    decoded = decoded.astype(BF16).astype(F32)
    acceleration = lax.dot_general(
        dw2_ref[...],
        decoded,
        (((1,), (1,)), ((), ())),
        precision=lax.Precision.HIGHEST,
        preferred_element_type=F32,
    )
    state_rows, particles = kin_ref.shape
    velocity = kin_ref[state_rows - 3 :, :] + acceleration
    state = jnp.concatenate([kin_ref[:3, :] + velocity, kin_ref[6:, :], velocity], axis=0)
    direction = leave_ref[0:1, :]
    staying = direction == 13
    stayed_ref[...] = jnp.where(staying, state, 0.0)
    dx, dy, dz = split_direction(direction)
    code = (dz * 9 + dx * 3 + dy) * MIG + leave_ref[1:2, :]
    code = jnp.where(staying, -1, code)
    picker = jnp.where(
        code == lax.broadcasted_iota(jnp.int32, (27 * MIG, particles), 0), 1.0, 0.0
    )
    outgoing = lax.dot_general(
        picker,
        state,
        (((1,), (1,)), ((), ())),
        precision=lax.Precision.HIGHEST,
        preferred_element_type=F32,
    )
    step = 9 * MIG
    for index, out in enumerate((low, mid, high)):
        out[...] = outgoing[index * step : (index + 1) * step]


def whole(shape):
    return pl.BlockSpec(shape, lambda i: (0,) * len(shape))


def call(body, args, specs, outs, name, flops=0, moved=0):
    return pl.pallas_call(
        body,
        grid=(1,),
        in_specs=[spec if spec is not None else whole(a.shape) for a, spec in zip(args, specs)],
        out_specs=[whole(s.shape) for s in outs],
        out_shape=outs,
        compiler_params=pltpu.CompilerParams(vmem_limit_bytes=VMEM_LIMIT),
        cost_estimate=pl.CostEstimate(flops=flops, bytes_accessed=moved, transcendentals=0),
        name=name,
    )(*args)


def shape(dims, dtype):
    return jax.ShapeDtypeStruct(dims, dtype)


def swapped(value, axis, first):
    pairs = []
    for low in range(first, lax.axis_size(axis) - 1, 2):
        pairs += [(low, low + 1), (low + 1, low)]
    return lax.ppermute(value, axis, pairs)


def moved_in_pairs(low, mid, high, axis):
    even = lax.axis_index(axis) % 2 == 0
    odd_pairs = swapped(jnp.where(even, low, high), axis, 1)
    even_pairs = swapped(jnp.where(even, high, low), axis, 0)
    from_below = jnp.where(even, odd_pairs, even_pairs)
    from_above = jnp.where(even, even_pairs, odd_pairs)
    return [from_below, mid, from_above]


def moved(low, mid, high, axis):
    return [shifted(high, axis, 1), mid, shifted(low, axis, -1)]


def exchanged(low, mid, high, rows):
    tail = low.shape[-1]
    parts = moved_in_pairs(low, mid, high, "gz")
    parts = [part.reshape(3, 3 * rows, tail) for part in parts]
    parts = moved(*(jnp.concatenate([part[x] for part in parts], axis=0) for x in range(3)), "gx")
    parts = [part.reshape(3, 3, rows, tail) for part in parts]
    low, mid, high = (
        jnp.stack([part[:, y] for part in parts], axis=1).reshape(9 * rows, tail)
        for y in range(3)
    )
    return moved(low, mid, high, "gy")


def on_device(
    kinematics,
    pair_offsets,
    pair_index,
    neighbour_count,
    send_rows,
    migrate_dir,
    migrate_slot,
    enc_node_w1,
    enc_node_w2,
    enc_edge_w1,
    enc_edge_w2,
    edge_w1,
    edge_w2,
    node_w1,
    node_w2,
    edge_gain,
    node_gain,
    dec_w1,
    dec_w2,
):
    width = enc_node_w2.shape[1]
    slots, particles = pair_index.shape
    ghost_rows = send_rows.shape[1]
    rounds = edge_w1.shape[0]
    state_rows = kinematics.shape[0]
    rows = send_rows.T
    part = shape((9 * ghost_rows, width), BF16)
    latent, low, mid, high = call(
        node_kernel,
        (kinematics, enc_node_w1, enc_node_w2, rows),
        (None,) * 4,
        [shape((particles, width), BF16), part, part, part],
        "node_encoder",
    )
    edges, columns = call(
        edge_kernel,
        (
            pair_offsets,
            pair_index,
            neighbour_count.reshape(1, particles),
            enc_edge_w1,
            enc_edge_w2,
        ),
        (None,) * 5,
        [shape((slots, particles, width), BF16), shape((particles, 128), jnp.int32)],
        "edge_encoder",
        flops=2 * slots * particles * 256 * 384,
        moved=4 * slots * particles * width,
    )
    leaving = jnp.stack([migrate_dir, migrate_slot], axis=0)
    for r in range(rounds):
        ghosts = exchanged(low, mid, high, ghost_rows)

        def of_round(array):
            return pl.BlockSpec((1,) + array.shape[1:], lambda i: (r, 0, 0))

        (part_sum,) = call(
            local_kernel,
            (latent, edges, columns, edge_w1),
            (None, None, None, of_round(edge_w1)),
            [shape((slots, particles, width), F32)],
            "local_pairs",
            flops=2 * slots * particles * 256 * 512,
            moved=8 * slots * particles * width,
        )
        weights = [edge_w1, edge_w2, node_w1, node_w2]
        args = [latent, *ghosts, part_sum, columns, *weights, edge_gain, node_gain]
        specs = [None] * 6 + [of_round(w) for w in weights] + [None, None]
        if r < rounds - 1:
            latent, low, mid, high = call(
                functools.partial(round_kernel, r),
                args + [rows],
                specs + [None],
                [shape((particles, width), BF16), part, part, part],
                "message_round",
            )
        else:
            out = shape((9 * MIG, state_rows), F32)
            stayed, low, mid, high = call(
                functools.partial(last_kernel, r),
                args + [kinematics, leaving, dec_w1, dec_w2],
                specs + [None] * 4,
                [shape((state_rows, particles), F32), out, out, out],
                "last_round",
            )
    landed = jnp.stack(exchanged(low, mid, high, MIG), axis=0)
    landed = landed.reshape(3, 3, 3, MIG, state_rows).transpose(4, 2, 0, 1, 3)
    return (stayed, landed.reshape(state_rows, 27 * MIG))


def solution(mesh):
    axes = ("gx", "gy", "gz")
    return jax.shard_map(
        on_device,
        mesh=mesh,
        in_specs=(
            P(None, axes),
            P(None, None, axes),
            P(None, axes),
            P(axes),
            P(None, axes),
            P(axes),
            P(axes),
        )
        + (P(),) * 12,
        out_specs=(P(None, axes), P(None, axes)),
        check_vma=False,
    )
```

```python
import functools

import jax
import jax.numpy as jnp
from jax import lax
from jax.experimental import pallas as pl
from jax.experimental.pallas import tpu as pltpu
from jax.sharding import PartitionSpec as P

MIG = 4
BLOCK = 8
EPS = 1e-05
F32 = jnp.float32
BF16 = jnp.bfloat16
VMEM_LIMIT = 48 * 1024 * 1024
FETCH_LIMIT = 60 * 1024 * 1024


def shifted(value, axis, steps):
    count = lax.axis_size(axis)
    first, last = (max(0, -steps), min(count, count - steps))
    return lax.ppermute(value, axis, [(source, source + steps) for source in range(first, last)])


def mm(a, b):
    return jnp.dot(a, b, preferred_element_type=F32)


def halves(value):
    high = value.astype(BF16)
    return high, (value - high.astype(F32)).astype(BF16)


def centred(weight):
    wide = weight.astype(F32)
    wide = wide - jnp.mean(wide, axis=-1, keepdims=True)
    return jnp.concatenate(halves(wide), axis=1)


def normalised(rows, weight):
    both = mm(rows, weight)
    width = both.shape[1] // 2
    center = both[:, :width] + both[:, width:]
    spread = jnp.mean(center * center, axis=-1, keepdims=True)
    return center, lax.rsqrt(spread + EPS)


def send_rows_of(latent, rows_ref, outs):
    particles = latent.shape[0]
    depth = rows_ref.shape[0]
    lanes = lax.broadcasted_iota(jnp.int32, (depth, particles), 1)
    for z, out in enumerate(outs):
        picked = [
            jnp.where(rows_ref[:, d : d + 1] == lanes, 1.0, 0.0)
            for d in [x * 9 + y * 3 + z for x in range(3) for y in range(3)]
        ]
        picked = jnp.concatenate(picked, axis=0).astype(BF16)
        out[...] = mm(picked, latent).astype(BF16)


def split_direction(direction):
    dx = (direction * 57) >> 9
    rest = direction - dx * 9
    dy = (rest * 11) >> 5
    return dx, dy, rest - dy * 3


def node_kernel(kin_ref, w1_ref, w2_ref, rows_ref, latent_ref, low_ref, mid_ref, high_ref):
    features = kin_ref[3:, :]
    hidden = lax.dot_general(
        features,
        w1_ref[...],
        (((0,), (0,)), ((), ())),
        precision=lax.Precision.HIGHEST,
        preferred_element_type=F32,
    )
    hidden = jnp.maximum(hidden, 0.0).astype(BF16)
    center, scale = normalised(hidden, centred(w2_ref[...]))
    latent = (center * scale).astype(BF16)
    latent_ref[...] = latent
    send_rows_of(latent, rows_ref, (low_ref, mid_ref, high_ref))


def edge_kernel(off_ref, index_ref, count_ref, w1_ref, w2_ref, edge_ref, column_ref):
    slots, particles = index_ref.shape
    index = index_ref[...]
    place = index - particles
    slot = place & 15
    dx, dy, dz = split_direction(place >> 4)
    moved = particles + (dy * 9 + dz * 3 + dx) * 16 + slot
    index = jnp.where(index < particles, index, moved).astype(F32)
    count = count_ref[...].astype(F32)
    filler = jnp.zeros((128 - slots - count.shape[0], particles), F32)
    column_ref[...] = jnp.concatenate([index, count, filler], axis=0).T.astype(jnp.int32)

    offsets = [off_ref[c] for c in range(3)]
    square = offsets[0] * offsets[0] + offsets[1] * offsets[1] + offsets[2] * offsets[2]
    stack = jnp.concatenate(offsets + [square], axis=0)
    high = stack.astype(BF16).astype(F32)
    low = stack - high
    wide = jnp.concatenate([high, low, high, jnp.zeros_like(high)], axis=0).T.astype(BF16)
    first = w1_ref[...]
    width = first.shape[1]
    first_high = first.astype(BF16).astype(F32)
    first_low = first - first_high
    rows = [
        jnp.broadcast_to(part[c : c + 1], (slots, width))
        for part in (first_high, first_high, first_low, jnp.zeros_like(first))
        for c in range(4)
    ]
    table = jnp.concatenate(rows, axis=0)
    owner = lax.broadcasted_iota(jnp.int32, table.shape, 0) & (slots - 1)
    second = centred(w2_ref[...])
    for k in range(slots):
        chosen = jnp.where(owner == k, table, 0.0).astype(BF16)
        hidden = jnp.maximum(mm(wide, chosen), 0.0).astype(BF16)
        center, scale = normalised(hidden, second)
        edge_ref[k] = (center * scale).astype(BF16)


def one_hot(column_ref, first, count, lanes):
    picked = [
        jnp.where(column_ref[:, k : k + 1] == lanes, 1.0, 0.0).astype(BF16)
        for k in range(first, first + count)
    ]
    return jnp.concatenate(picked, axis=0)


def local_kernel(latent_ref, edge_ref, column_ref, w1_ref, *refs):
    out_ref = refs[-1]
    slots, particles, width = edge_ref.shape
    latent = latent_ref[...]
    receiver = mm(latent, w1_ref[0, width : 2 * width])
    sender = jnp.concatenate(halves(mm(latent, w1_ref[0, 2 * width :])), axis=1)
    first = w1_ref[0, :width]
    lanes = lax.broadcasted_iota(jnp.int32, (particles, particles), 1)
    for k in range(0, slots, BLOCK):
        both = mm(one_hot(column_ref, k, BLOCK, lanes), sender)
        pre = mm(edge_ref[k : k + BLOCK].reshape(BLOCK * particles, width), first)
        pre = pre + both[:, :width] + both[:, width:]
        for j in range(BLOCK):
            out_ref[k + j] = pre[j * particles : (j + 1) * particles] + receiver


def updated_latent(r, latent_ref, ghost_refs, part_ref, column_ref, refs):
    ew1_ref, ew2_ref, nw1_ref, nw2_ref, eg_ref, ng_ref = refs
    latent = latent_ref[...]
    slots, particles, width = part_ref.shape
    total = sum(ref.shape[0] for ref in ghost_refs)
    padded = -(-total // 256) * 256
    filler = jnp.zeros((padded - total, width), BF16)
    ghosts = jnp.concatenate([ref[...] for ref in ghost_refs] + [filler], axis=0)
    sender = jnp.concatenate(halves(mm(ghosts, ew1_ref[0, 2 * width :])), axis=1)
    second = centred(ew2_ref[0])
    lanes = lax.broadcasted_iota(jnp.int32, (particles, padded), 1) + particles
    counts = jnp.broadcast_to(column_ref[:, slots : slots + 1], (particles, width))
    summed = jnp.zeros((particles, width), F32)
    for k in range(0, slots, BLOCK):
        both = mm(one_hot(column_ref, k, BLOCK, lanes), sender)
        pre = part_ref[k : k + BLOCK].reshape(BLOCK * particles, width)
        pre = pre + both[:, :width] + both[:, width:]
        hidden = jnp.maximum(pre, 0.0).astype(BF16)
        center, scale = normalised(hidden, second)
        message = center * scale
        for j in range(BLOCK):
            rows = slice(j * particles, (j + 1) * particles)
            summed = summed + jnp.where(counts > k + j, message[rows], 0.0)
    aggregate = (summed * eg_ref[r : r + 1]).astype(BF16)
    node_pre = mm(jnp.concatenate([latent, aggregate], axis=1), nw1_ref[0])
    node_mid = jnp.maximum(node_pre, 0.0).astype(BF16)
    center, scale = normalised(node_mid, centred(nw2_ref[0]))
    update = center * scale * ng_ref[r : r + 1]
    return (latent.astype(F32) + update).astype(BF16)


def round_kernel(r, latent_ref, g0, g1, g2, part_ref, column_ref, *refs):
    rows_ref, out_ref, low, mid, high = refs[6:]
    latent = updated_latent(r, latent_ref, (g0, g1, g2), part_ref, column_ref, refs[:6])
    out_ref[...] = latent
    send_rows_of(latent, rows_ref, (low, mid, high))


def last_kernel(r, latent_ref, g0, g1, g2, part_ref, column_ref, *refs):
    kin_ref, dir_ref, slot_ref, dw1_ref, dw2_ref, stayed_ref, low, mid, high = refs[6:]
    latent = updated_latent(r, latent_ref, (g0, g1, g2), part_ref, column_ref, refs[:6])
    decoded = jnp.maximum(mm(latent, dw1_ref[...]), 0.0)
    decoded = decoded.astype(BF16).astype(F32)
    acceleration = lax.dot_general(
        dw2_ref[...],
        decoded,
        (((1,), (1,)), ((), ())),
        precision=lax.Precision.HIGHEST,
        preferred_element_type=F32,
    )
    state_rows, particles = kin_ref.shape
    velocity = kin_ref[state_rows - 3 :, :] + acceleration
    state = jnp.concatenate([kin_ref[:3, :] + velocity, kin_ref[6:, :], velocity], axis=0)
    direction = dir_ref[...]
    staying = direction == 13
    stayed_ref[...] = jnp.where(staying, state, 0.0)
    dx, dy, dz = split_direction(direction)
    code = (dz * 9 + dx * 3 + dy) * MIG + slot_ref[...]
    code = jnp.where(staying, -1, code)
    picker = jnp.where(
        code == lax.broadcasted_iota(jnp.int32, (27 * MIG, particles), 0), 1.0, 0.0
    )
    outgoing = lax.dot_general(
        picker,
        state,
        (((1,), (1,)), ((), ())),
        precision=lax.Precision.HIGHEST,
        preferred_element_type=F32,
    )
    step = 9 * MIG
    for index, out in enumerate((low, mid, high)):
        out[...] = outgoing[index * step : (index + 1) * step]


def whole(shape):
    return pl.BlockSpec(shape, lambda i: (0,) * len(shape))


def call(body, args, specs, outs, name, flops=0, moved=0):
    return pl.pallas_call(
        body,
        grid=(1,),
        in_specs=[spec if spec is not None else whole(a.shape) for a, spec in zip(args, specs)],
        out_specs=[whole(s.shape) for s in outs],
        out_shape=outs,
        compiler_params=pltpu.CompilerParams(vmem_limit_bytes=VMEM_LIMIT),
        cost_estimate=pl.CostEstimate(flops=flops, bytes_accessed=moved, transcendentals=0),
        name=name,
    )(*args)


def fetching(body, count, *refs):
    sources, outs = refs[:count], refs[count : -count - 1]
    targets, sems = refs[-count - 1 : -1], refs[-1]
    copies = [
        pltpu.make_async_copy(source, target, sems.at[i])
        for i, (source, target) in enumerate(zip(sources, targets))
    ]
    for copy in copies:
        copy.start()
    for copy in copies:
        copy.wait()
    body(*targets, *outs)


def call_fetching(body, args, outs, name, flops=0, moved=0):
    return pl.pallas_call(
        functools.partial(fetching, body, len(args)),
        in_specs=[pl.BlockSpec(memory_space=pltpu.HBM)] * len(args),
        out_specs=[pl.BlockSpec(memory_space=pltpu.VMEM)] * len(outs),
        out_shape=outs,
        scratch_shapes=[pltpu.VMEM(a.shape, a.dtype) for a in args]
        + [pltpu.SemaphoreType.DMA((len(args),))],
        compiler_params=pltpu.CompilerParams(vmem_limit_bytes=FETCH_LIMIT),
        cost_estimate=pl.CostEstimate(flops=flops, bytes_accessed=moved, transcendentals=0),
        name=name,
    )(*args)


def shape(dims, dtype):
    return jax.ShapeDtypeStruct(dims, dtype)


def swapped(value, axis, first):
    pairs = []
    for low in range(first, lax.axis_size(axis) - 1, 2):
        pairs += [(low, low + 1), (low + 1, low)]
    return lax.ppermute(value, axis, pairs)


def moved_in_pairs(low, mid, high, axis):
    even = lax.axis_index(axis) % 2 == 0
    odd_pairs = swapped(jnp.where(even, low, high), axis, 1)
    even_pairs = swapped(jnp.where(even, high, low), axis, 0)
    from_below = jnp.where(even, odd_pairs, even_pairs)
    from_above = jnp.where(even, even_pairs, odd_pairs)
    return [from_below, mid, from_above]


def moved(low, mid, high, axis):
    return [shifted(high, axis, 1), mid, shifted(low, axis, -1)]


def exchanged(low, mid, high, rows):
    tail = low.shape[-1]
    parts = moved_in_pairs(low, mid, high, "gz")
    hold = parts[0]
    parts = [part.reshape(3, 3 * rows, tail) for part in parts]
    parts = moved(*(jnp.concatenate([part[x] for part in parts], axis=0) for x in range(3)), "gx")
    parts = [part.reshape(3, 3, rows, tail) for part in parts]
    low, mid, high = (
        jnp.stack([part[:, y] for part in parts], axis=1).reshape(9 * rows, tail)
        for y in range(3)
    )
    return moved(low, mid, high, "gy"), hold


def on_device(
    kinematics,
    pair_offsets,
    pair_index,
    neighbour_count,
    send_rows,
    migrate_dir,
    migrate_slot,
    enc_node_w1,
    enc_node_w2,
    enc_edge_w1,
    enc_edge_w2,
    edge_w1,
    edge_w2,
    node_w1,
    node_w2,
    edge_gain,
    node_gain,
    dec_w1,
    dec_w2,
):
    width = enc_node_w2.shape[1]
    slots, particles = pair_index.shape
    ghost_rows = send_rows.shape[1]
    rounds = edge_w1.shape[0]
    state_rows = kinematics.shape[0]
    rows = send_rows.T
    part = shape((9 * ghost_rows, width), BF16)
    latent, low, mid, high = call_fetching(
        node_kernel,
        (kinematics, enc_node_w1, enc_node_w2, rows),
        [shape((particles, width), BF16), part, part, part],
        "node_encoder",
    )
    edges, columns = call_fetching(
        edge_kernel,
        (
            pair_offsets,
            pair_index,
            neighbour_count.reshape(1, particles),
            enc_edge_w1,
            enc_edge_w2,
        ),
        [shape((slots, particles, width), BF16), shape((particles, 128), jnp.int32)],
        "edge_encoder",
        flops=2 * slots * particles * 256 * 384,
        moved=4 * slots * particles * width,
    )
    leaving = [migrate_dir.reshape(1, particles), migrate_slot.reshape(1, particles)]
    for r in range(rounds):
        ghosts, hold = exchanged(low, mid, high, ghost_rows)

        def of_round(array):
            return pl.BlockSpec((1,) + array.shape[1:], lambda i: (r, 0, 0))

        held = (hold,) if r == 0 else ()
        (part_sum,) = call(
            local_kernel,
            (latent, edges, columns, edge_w1) + held,
            (None, None, None, of_round(edge_w1)) + (None,) * len(held),
            [shape((slots, particles, width), F32)],
            "local_pairs",
            flops=2 * slots * particles * 256 * 512,
            moved=8 * slots * particles * width,
        )
        weights = [edge_w1, edge_w2, node_w1, node_w2]
        args = [latent, *ghosts, part_sum, columns, *weights, edge_gain, node_gain]
        specs = [None] * 6 + [of_round(w) for w in weights] + [None, None]
        if r < rounds - 1:
            latent, low, mid, high = call(
                functools.partial(round_kernel, r),
                args + [rows],
                specs + [None],
                [shape((particles, width), BF16), part, part, part],
                "message_round",
            )
        else:
            out = shape((9 * MIG, state_rows), F32)
            stayed, low, mid, high = call(
                functools.partial(last_kernel, r),
                args + [kinematics, *leaving, dec_w1, dec_w2],
                specs + [None] * 5,
                [shape((state_rows, particles), F32), out, out, out],
                "last_round",
            )
    landed = jnp.stack(exchanged(low, mid, high, MIG)[0], axis=0)
    landed = landed.reshape(3, 3, 3, MIG, state_rows).transpose(4, 2, 0, 1, 3)
    return (stayed, landed.reshape(state_rows, 27 * MIG))


def solution(mesh):
    axes = ("gx", "gy", "gz")
    return jax.shard_map(
        on_device,
        mesh=mesh,
        in_specs=(
            P(None, axes),
            P(None, None, axes),
            P(None, axes),
            P(axes),
            P(None, axes),
            P(axes),
            P(axes),
        )
        + (P(),) * 12,
        out_specs=(P(None, axes), P(None, axes)),
        check_vma=False,
    )
```

```python
import functools

import jax
import jax.numpy as jnp
from jax import lax
from jax.experimental import pallas as pl
from jax.experimental.pallas import tpu as pltpu
from jax.sharding import PartitionSpec as P

MIG = 4
BLOCK = 8
EPS = 1e-05
F32 = jnp.float32
BF16 = jnp.bfloat16
VMEM_LIMIT = 48 * 1024 * 1024
FETCH_LIMIT = 60 * 1024 * 1024


def shifted(value, axis, steps):
    count = lax.axis_size(axis)
    first, last = (max(0, -steps), min(count, count - steps))
    return lax.ppermute(value, axis, [(source, source + steps) for source in range(first, last)])


def mm(a, b):
    return jnp.dot(a, b, preferred_element_type=F32)


def halves(value):
    high = value.astype(BF16)
    return high, (value - high.astype(F32)).astype(BF16)


def centred(weight):
    wide = weight.astype(F32)
    wide = wide - jnp.mean(wide, axis=-1, keepdims=True)
    return jnp.concatenate(halves(wide), axis=1)


def normalised(rows, weight):
    both = mm(rows, weight)
    width = both.shape[1] // 2
    center = both[:, :width] + both[:, width:]
    spread = jnp.mean(center * center, axis=-1, keepdims=True)
    return center, lax.rsqrt(spread + EPS)


def by_parity(rows, outs):
    even = lax.axis_index("gz") % 2 == 0
    low, mid, high = rows
    odd_ref, mid_ref, even_ref = outs
    mid_ref[...] = mid

    @pl.when(even)
    def _():
        odd_ref[...] = low
        even_ref[...] = high

    @pl.when(jnp.logical_not(even))
    def _():
        odd_ref[...] = high
        even_ref[...] = low


def send_rows_of(latent, rows_ref, outs):
    particles = latent.shape[0]
    depth = rows_ref.shape[0]
    lanes = lax.broadcasted_iota(jnp.int32, (depth, particles), 1)
    chosen = []
    for z in range(3):
        picked = [
            jnp.where(rows_ref[:, d : d + 1] == lanes, 1.0, 0.0)
            for d in [x * 9 + y * 3 + z for x in range(3) for y in range(3)]
        ]
        picked = jnp.concatenate(picked, axis=0).astype(BF16)
        chosen.append(mm(picked, latent).astype(BF16))
    by_parity(chosen, outs)


def split_direction(direction):
    dx = (direction * 57) >> 9
    rest = direction - dx * 9
    dy = (rest * 11) >> 5
    return dx, dy, rest - dy * 3


def node_kernel(kin_ref, w1_ref, w2_ref, rows_ref, latent_ref, low_ref, mid_ref, high_ref):
    features = kin_ref[3:, :]
    hidden = lax.dot_general(
        features,
        w1_ref[...],
        (((0,), (0,)), ((), ())),
        precision=lax.Precision.HIGHEST,
        preferred_element_type=F32,
    )
    hidden = jnp.maximum(hidden, 0.0).astype(BF16)
    center, scale = normalised(hidden, centred(w2_ref[...]))
    latent = (center * scale).astype(BF16)
    latent_ref[...] = latent
    send_rows_of(latent, rows_ref, (low_ref, mid_ref, high_ref))


def edge_kernel(off_ref, index_ref, count_ref, w1_ref, w2_ref, edge_ref, column_ref):
    slots, particles = index_ref.shape
    index = index_ref[...]
    place = index - particles
    slot = place & 15
    dx, dy, dz = split_direction(place >> 4)
    moved = particles + (dy * 9 + dz * 3 + dx) * 16 + slot
    index = jnp.where(index < particles, index, moved).astype(F32)
    count = count_ref[...].astype(F32)
    filler = jnp.zeros((128 - slots - count.shape[0], particles), F32)
    column_ref[...] = jnp.concatenate([index, count, filler], axis=0).T.astype(jnp.int32)

    offsets = [off_ref[c] for c in range(3)]
    square = offsets[0] * offsets[0] + offsets[1] * offsets[1] + offsets[2] * offsets[2]
    stack = jnp.concatenate(offsets + [square], axis=0)
    high = stack.astype(BF16).astype(F32)
    low = stack - high
    wide = jnp.concatenate([high, low, high, jnp.zeros_like(high)], axis=0).T.astype(BF16)
    first = w1_ref[...]
    width = first.shape[1]
    first_high = first.astype(BF16).astype(F32)
    first_low = first - first_high
    rows = [
        jnp.broadcast_to(part[c : c + 1], (slots, width))
        for part in (first_high, first_high, first_low, jnp.zeros_like(first))
        for c in range(4)
    ]
    table = jnp.concatenate(rows, axis=0)
    owner = lax.broadcasted_iota(jnp.int32, table.shape, 0) & (slots - 1)
    second = centred(w2_ref[...])
    for k in range(slots):
        chosen = jnp.where(owner == k, table, 0.0).astype(BF16)
        hidden = jnp.maximum(mm(wide, chosen), 0.0).astype(BF16)
        center, scale = normalised(hidden, second)
        edge_ref[k] = (center * scale).astype(BF16)


def one_hot(column_ref, first, count, lanes):
    picked = [
        jnp.where(column_ref[:, k : k + 1] == lanes, 1.0, 0.0).astype(BF16)
        for k in range(first, first + count)
    ]
    return jnp.concatenate(picked, axis=0)


def local_kernel(latent_ref, edge_ref, column_ref, w1_ref, *refs):
    out_ref = refs[-1]
    slots, particles, width = edge_ref.shape
    latent = latent_ref[...]
    receiver = mm(latent, w1_ref[0, width : 2 * width])
    sender = jnp.concatenate(halves(mm(latent, w1_ref[0, 2 * width :])), axis=1)
    first = w1_ref[0, :width]
    lanes = lax.broadcasted_iota(jnp.int32, (particles, particles), 1)
    for k in range(0, slots, BLOCK):
        both = mm(one_hot(column_ref, k, BLOCK, lanes), sender)
        pre = mm(edge_ref[k : k + BLOCK].reshape(BLOCK * particles, width), first)
        pre = pre + both[:, :width] + both[:, width:]
        for j in range(BLOCK):
            out_ref[k + j] = pre[j * particles : (j + 1) * particles] + receiver


def updated_latent(r, latent_ref, ghost_refs, part_ref, column_ref, refs):
    ew1_ref, ew2_ref, nw1_ref, nw2_ref, eg_ref, ng_ref = refs
    latent = latent_ref[...]
    slots, particles, width = part_ref.shape
    total = sum(ref.shape[0] for ref in ghost_refs)
    padded = -(-total // 256) * 256
    filler = jnp.zeros((padded - total, width), BF16)
    ghosts = jnp.concatenate([ref[...] for ref in ghost_refs] + [filler], axis=0)
    sender = jnp.concatenate(halves(mm(ghosts, ew1_ref[0, 2 * width :])), axis=1)
    second = centred(ew2_ref[0])
    lanes = lax.broadcasted_iota(jnp.int32, (particles, padded), 1) + particles
    counts = jnp.broadcast_to(column_ref[:, slots : slots + 1], (particles, width))
    summed = jnp.zeros((particles, width), F32)
    for k in range(0, slots, BLOCK):
        both = mm(one_hot(column_ref, k, BLOCK, lanes), sender)
        pre = part_ref[k : k + BLOCK].reshape(BLOCK * particles, width)
        pre = pre + both[:, :width] + both[:, width:]
        hidden = jnp.maximum(pre, 0.0).astype(BF16)
        center, scale = normalised(hidden, second)
        message = center * scale
        for j in range(BLOCK):
            rows = slice(j * particles, (j + 1) * particles)
            summed = summed + jnp.where(counts > k + j, message[rows], 0.0)
    aggregate = (summed * eg_ref[r : r + 1]).astype(BF16)
    node_pre = mm(jnp.concatenate([latent, aggregate], axis=1), nw1_ref[0])
    node_mid = jnp.maximum(node_pre, 0.0).astype(BF16)
    center, scale = normalised(node_mid, centred(nw2_ref[0]))
    update = center * scale * ng_ref[r : r + 1]
    return (latent.astype(F32) + update).astype(BF16)


def round_kernel(r, latent_ref, g2, g1, g0, part_ref, column_ref, *refs):
    rows_ref, out_ref, low, mid, high = refs[6:]
    latent = updated_latent(r, latent_ref, (g0, g1, g2), part_ref, column_ref, refs[:6])
    out_ref[...] = latent
    send_rows_of(latent, rows_ref, (low, mid, high))


def last_kernel(r, latent_ref, g2, g1, g0, part_ref, column_ref, *refs):
    kin_ref, dir_ref, slot_ref, dw1_ref, dw2_ref, stayed_ref, low, mid, high = refs[6:]
    latent = updated_latent(r, latent_ref, (g0, g1, g2), part_ref, column_ref, refs[:6])
    decoded = jnp.maximum(mm(latent, dw1_ref[...]), 0.0)
    decoded = decoded.astype(BF16).astype(F32)
    acceleration = lax.dot_general(
        dw2_ref[...],
        decoded,
        (((1,), (1,)), ((), ())),
        precision=lax.Precision.HIGHEST,
        preferred_element_type=F32,
    )
    state_rows, particles = kin_ref.shape
    velocity = kin_ref[state_rows - 3 :, :] + acceleration
    state = jnp.concatenate([kin_ref[:3, :] + velocity, kin_ref[6:, :], velocity], axis=0)
    direction = dir_ref[...]
    staying = direction == 13
    stayed_ref[...] = jnp.where(staying, state, 0.0)
    dx, dy, dz = split_direction(direction)
    code = (dz * 9 + dx * 3 + dy) * MIG + slot_ref[...]
    code = jnp.where(staying, -1, code)
    picker = jnp.where(
        code == lax.broadcasted_iota(jnp.int32, (27 * MIG, particles), 0), 1.0, 0.0
    )
    outgoing = lax.dot_general(
        picker,
        state,
        (((1,), (1,)), ((), ())),
        precision=lax.Precision.HIGHEST,
        preferred_element_type=F32,
    )
    step = 9 * MIG
    by_parity([outgoing[i * step : (i + 1) * step] for i in range(3)], (low, mid, high))


def whole(shape):
    return pl.BlockSpec(shape, lambda i: (0,) * len(shape))


def call(body, args, specs, outs, name, flops=0, moved=0):
    return pl.pallas_call(
        body,
        grid=(1,),
        in_specs=[spec if spec is not None else whole(a.shape) for a, spec in zip(args, specs)],
        out_specs=[whole(s.shape) for s in outs],
        out_shape=outs,
        compiler_params=pltpu.CompilerParams(vmem_limit_bytes=VMEM_LIMIT),
        cost_estimate=pl.CostEstimate(flops=flops, bytes_accessed=moved, transcendentals=0),
        name=name,
    )(*args)


def fetching(body, count, *refs):
    sources, outs = refs[:count], refs[count : -count - 1]
    targets, sems = refs[-count - 1 : -1], refs[-1]
    copies = [
        pltpu.make_async_copy(source, target, sems.at[i])
        for i, (source, target) in enumerate(zip(sources, targets))
    ]
    for copy in copies:
        copy.start()
    for copy in copies:
        copy.wait()
    body(*targets, *outs)


def call_fetching(body, args, outs, name, flops=0, moved=0):
    return pl.pallas_call(
        functools.partial(fetching, body, len(args)),
        in_specs=[pl.BlockSpec(memory_space=pltpu.HBM)] * len(args),
        out_specs=[pl.BlockSpec(memory_space=pltpu.VMEM)] * len(outs),
        out_shape=outs,
        scratch_shapes=[pltpu.VMEM(a.shape, a.dtype) for a in args]
        + [pltpu.SemaphoreType.DMA((len(args),))],
        compiler_params=pltpu.CompilerParams(vmem_limit_bytes=FETCH_LIMIT),
        cost_estimate=pl.CostEstimate(flops=flops, bytes_accessed=moved, transcendentals=0),
        name=name,
    )(*args)


def shape(dims, dtype):
    return jax.ShapeDtypeStruct(dims, dtype)


def swapped(value, axis, first):
    pairs = []
    for low in range(first, lax.axis_size(axis) - 1, 2):
        pairs += [(low, low + 1), (low + 1, low)]
    return lax.ppermute(value, axis, pairs)


def moved_in_pairs(to_odd, mid, to_even, axis):
    even = lax.axis_index(axis) % 2 == 0
    odd_pairs = swapped(to_odd, axis, 1)
    even_pairs = swapped(to_even, axis, 0)
    from_below = jnp.where(even, odd_pairs, even_pairs)
    from_above = jnp.where(even, even_pairs, odd_pairs)
    return [from_below, mid, from_above]


def moved(low, mid, high, axis):
    return [shifted(high, axis, 1), mid, shifted(low, axis, -1)]


def exchanged(low, mid, high, rows):
    tail = low.shape[-1]
    parts = moved_in_pairs(low, mid, high, "gz")
    hold = parts[0]
    parts = [part.reshape(3, 3 * rows, tail) for part in parts]
    parts = moved(*(jnp.concatenate([part[x] for part in parts], axis=0) for x in range(3)), "gx")
    parts = [part.reshape(3, 3, rows, tail) for part in parts]
    low, mid, high = (
        jnp.stack([part[:, y] for part in parts], axis=1).reshape(9 * rows, tail)
        for y in range(3)
    )
    return moved(low, mid, high, "gy"), hold


def on_device(
    kinematics,
    pair_offsets,
    pair_index,
    neighbour_count,
    send_rows,
    migrate_dir,
    migrate_slot,
    enc_node_w1,
    enc_node_w2,
    enc_edge_w1,
    enc_edge_w2,
    edge_w1,
    edge_w2,
    node_w1,
    node_w2,
    edge_gain,
    node_gain,
    dec_w1,
    dec_w2,
):
    width = enc_node_w2.shape[1]
    slots, particles = pair_index.shape
    ghost_rows = send_rows.shape[1]
    rounds = edge_w1.shape[0]
    state_rows = kinematics.shape[0]
    rows = send_rows.T
    part = shape((9 * ghost_rows, width), BF16)
    latent, low, mid, high = call_fetching(
        node_kernel,
        (kinematics, enc_node_w1, enc_node_w2, rows),
        [shape((particles, width), BF16), part, part, part],
        "node_encoder",
    )
    edges, columns = call_fetching(
        edge_kernel,
        (
            pair_offsets,
            pair_index,
            neighbour_count.reshape(1, particles),
            enc_edge_w1,
            enc_edge_w2,
        ),
        [shape((slots, particles, width), BF16), shape((particles, 128), jnp.int32)],
        "edge_encoder",
        flops=2 * slots * particles * 256 * 384,
        moved=4 * slots * particles * width,
    )
    leaving = [migrate_dir.reshape(1, particles), migrate_slot.reshape(1, particles)]
    for r in range(rounds):
        ghosts, hold = exchanged(low, mid, high, ghost_rows)

        def of_round(array):
            return pl.BlockSpec((1,) + array.shape[1:], lambda i: (r, 0, 0))

        held = (hold,) if r == 0 else ()
        (part_sum,) = call(
            local_kernel,
            (latent, edges, columns, edge_w1) + held,
            (None, None, None, of_round(edge_w1)) + (None,) * len(held),
            [shape((slots, particles, width), F32)],
            "local_pairs",
            flops=2 * slots * particles * 256 * 512,
            moved=8 * slots * particles * width,
        )
        weights = [edge_w1, edge_w2, node_w1, node_w2]
        args = [latent, *ghosts[::-1], part_sum, columns, *weights, edge_gain, node_gain]
        specs = [None] * 6 + [of_round(w) for w in weights] + [None, None]
        if r < rounds - 1:
            latent, low, mid, high = call(
                functools.partial(round_kernel, r),
                args + [rows],
                specs + [None],
                [shape((particles, width), BF16), part, part, part],
                "message_round",
            )
        else:
            out = shape((9 * MIG, state_rows), F32)
            stayed, low, mid, high = call(
                functools.partial(last_kernel, r),
                args + [kinematics, *leaving, dec_w1, dec_w2],
                specs + [None] * 5,
                [shape((state_rows, particles), F32), out, out, out],
                "last_round",
            )
    landed = jnp.stack(exchanged(low, mid, high, MIG)[0], axis=0)
    landed = landed.reshape(3, 3, 3, MIG, state_rows).transpose(4, 2, 0, 1, 3)
    return (stayed, landed.reshape(state_rows, 27 * MIG))


def solution(mesh):
    axes = ("gx", "gy", "gz")
    return jax.shard_map(
        on_device,
        mesh=mesh,
        in_specs=(
            P(None, axes),
            P(None, None, axes),
            P(None, axes),
            P(axes),
            P(None, axes),
            P(axes),
            P(axes),
        )
        + (P(),) * 12,
        out_specs=(P(None, axes), P(None, axes)),
        check_vma=False,
    )
```

```python
import functools

import jax
import jax.numpy as jnp
from jax import lax
from jax.experimental import pallas as pl
from jax.experimental.pallas import tpu as pltpu
from jax.sharding import PartitionSpec as P

MIG = 4
BLOCK = 16
EPS = 1e-05
F32 = jnp.float32
BF16 = jnp.bfloat16
VMEM_LIMIT = 48 * 1024 * 1024
FETCH_LIMIT = 60 * 1024 * 1024


def shifted(value, axis, steps):
    count = lax.axis_size(axis)
    first, last = (max(0, -steps), min(count, count - steps))
    return lax.ppermute(value, axis, [(source, source + steps) for source in range(first, last)])


def mm(a, b):
    return jnp.dot(a, b, preferred_element_type=F32)


def halves(value):
    high = value.astype(BF16)
    return high, (value - high.astype(F32)).astype(BF16)


def centred(weight):
    wide = weight.astype(F32)
    wide = wide - jnp.mean(wide, axis=-1, keepdims=True)
    return jnp.concatenate(halves(wide), axis=1)


def normalised(rows, weight):
    both = mm(rows, weight)
    width = both.shape[1] // 2
    center = both[:, :width] + both[:, width:]
    spread = jnp.mean(center * center, axis=-1, keepdims=True)
    return center, lax.rsqrt(spread + EPS)


def by_parity(rows, outs):
    even = lax.axis_index("gz") % 2 == 0
    low, mid, high = rows
    odd_ref, mid_ref, even_ref = outs
    mid_ref[...] = mid

    @pl.when(even)
    def _():
        odd_ref[...] = low
        even_ref[...] = high

    @pl.when(jnp.logical_not(even))
    def _():
        odd_ref[...] = high
        even_ref[...] = low


def send_rows_of(latent, rows_ref, outs):
    particles = latent.shape[0]
    depth = rows_ref.shape[0]
    lanes = lax.broadcasted_iota(jnp.int32, (depth, particles), 1)
    chosen = []
    for z in range(3):
        picked = [
            jnp.where(rows_ref[:, d : d + 1] == lanes, 1.0, 0.0)
            for d in [x * 9 + y * 3 + z for x in range(3) for y in range(3)]
        ]
        picked = jnp.concatenate(picked, axis=0).astype(BF16)
        chosen.append(mm(picked, latent).astype(BF16))
    by_parity(chosen, outs)


def split_direction(direction):
    dx = (direction * 57) >> 9
    rest = direction - dx * 9
    dy = (rest * 11) >> 5
    return dx, dy, rest - dy * 3


def node_kernel(kin_ref, w1_ref, w2_ref, rows_ref, latent_ref, low_ref, mid_ref, high_ref):
    features = kin_ref[3:, :]
    hidden = lax.dot_general(
        features,
        w1_ref[...],
        (((0,), (0,)), ((), ())),
        precision=lax.Precision.HIGHEST,
        preferred_element_type=F32,
    )
    hidden = jnp.maximum(hidden, 0.0).astype(BF16)
    center, scale = normalised(hidden, centred(w2_ref[...]))
    latent = (center * scale).astype(BF16)
    latent_ref[...] = latent
    send_rows_of(latent, rows_ref, (low_ref, mid_ref, high_ref))


def edge_kernel(off_ref, index_ref, count_ref, w1_ref, w2_ref, edge_ref, column_ref):
    slots, particles = index_ref.shape
    index = index_ref[...]
    place = index - particles
    slot = place & 15
    dx, dy, dz = split_direction(place >> 4)
    moved = particles + (dy * 9 + dz * 3 + dx) * 16 + slot
    index = jnp.where(index < particles, index, moved).astype(F32)
    count = count_ref[...].astype(F32)
    filler = jnp.zeros((128 - slots - count.shape[0], particles), F32)
    column_ref[...] = jnp.concatenate([index, count, filler], axis=0).T.astype(jnp.int32)

    offsets = [off_ref[c] for c in range(3)]
    square = offsets[0] * offsets[0] + offsets[1] * offsets[1] + offsets[2] * offsets[2]
    stack = jnp.concatenate(offsets + [square], axis=0)
    high = stack.astype(BF16).astype(F32)
    low = stack - high
    wide = jnp.concatenate([high, low, high, jnp.zeros_like(high)], axis=0).T.astype(BF16)
    first = w1_ref[...]
    width = first.shape[1]
    first_high = first.astype(BF16).astype(F32)
    first_low = first - first_high
    rows = [
        jnp.broadcast_to(part[c : c + 1], (slots, width))
        for part in (first_high, first_high, first_low, jnp.zeros_like(first))
        for c in range(4)
    ]
    table = jnp.concatenate(rows, axis=0)
    owner = lax.broadcasted_iota(jnp.int32, table.shape, 0) & (slots - 1)
    second = centred(w2_ref[...])
    for k in range(slots):
        chosen = jnp.where(owner == k, table, 0.0).astype(BF16)
        hidden = jnp.maximum(mm(wide, chosen), 0.0).astype(BF16)
        center, scale = normalised(hidden, second)
        edge_ref[k] = (center * scale).astype(BF16)


def one_hot(column_ref, first, count, lanes):
    picked = [
        jnp.where(column_ref[:, k : k + 1] == lanes, 1.0, 0.0).astype(BF16)
        for k in range(first, first + count)
    ]
    return jnp.concatenate(picked, axis=0)


def local_kernel(latent_ref, edge_ref, column_ref, w1_ref, *refs):
    out_ref = refs[-1]
    slots, particles, width = edge_ref.shape
    latent = latent_ref[...]
    receiver = mm(latent, w1_ref[0, width : 2 * width])
    sender = jnp.concatenate(halves(mm(latent, w1_ref[0, 2 * width :])), axis=1)
    first = w1_ref[0, :width]
    lanes = lax.broadcasted_iota(jnp.int32, (particles, particles), 1)
    for k in range(0, slots, BLOCK):
        both = mm(one_hot(column_ref, k, BLOCK, lanes), sender)
        pre = mm(edge_ref[k : k + BLOCK].reshape(BLOCK * particles, width), first)
        pre = pre + both[:, :width] + both[:, width:]
        for j in range(BLOCK):
            out_ref[k + j] = pre[j * particles : (j + 1) * particles] + receiver


def updated_latent(r, latent_ref, ghost_refs, part_ref, column_ref, refs):
    ew1_ref, ew2_ref, nw1_ref, nw2_ref, eg_ref, ng_ref = refs
    latent = latent_ref[...]
    slots, particles, width = part_ref.shape
    total = sum(ref.shape[0] for ref in ghost_refs)
    padded = -(-total // 256) * 256
    filler = jnp.zeros((padded - total, width), BF16)
    ghosts = jnp.concatenate([ref[...] for ref in ghost_refs] + [filler], axis=0)
    sender = jnp.concatenate(halves(mm(ghosts, ew1_ref[0, 2 * width :])), axis=1)
    second = centred(ew2_ref[0])
    lanes = lax.broadcasted_iota(jnp.int32, (particles, padded), 1) + particles
    counts = jnp.broadcast_to(column_ref[:, slots : slots + 1], (particles, width))
    summed = jnp.zeros((particles, width), F32)
    for k in range(0, slots, BLOCK):
        both = mm(one_hot(column_ref, k, BLOCK, lanes), sender)
        pre = part_ref[k : k + BLOCK].reshape(BLOCK * particles, width)
        pre = pre + both[:, :width] + both[:, width:]
        hidden = jnp.maximum(pre, 0.0).astype(BF16)
        center, scale = normalised(hidden, second)
        message = center * scale
        for j in range(BLOCK):
            rows = slice(j * particles, (j + 1) * particles)
            summed = summed + jnp.where(counts > k + j, message[rows], 0.0)
    aggregate = (summed * eg_ref[r : r + 1]).astype(BF16)
    node_pre = mm(jnp.concatenate([latent, aggregate], axis=1), nw1_ref[0])
    node_mid = jnp.maximum(node_pre, 0.0).astype(BF16)
    center, scale = normalised(node_mid, centred(nw2_ref[0]))
    update = center * scale * ng_ref[r : r + 1]
    return (latent.astype(F32) + update).astype(BF16)


def round_kernel(r, latent_ref, g2, g1, g0, part_ref, column_ref, *refs):
    rows_ref, out_ref, low, mid, high = refs[6:]
    latent = updated_latent(r, latent_ref, (g0, g1, g2), part_ref, column_ref, refs[:6])
    out_ref[...] = latent
    send_rows_of(latent, rows_ref, (low, mid, high))


def last_kernel(r, latent_ref, g2, g1, g0, part_ref, column_ref, *refs):
    kin_ref, dir_ref, slot_ref, dw1_ref, dw2_ref, stayed_ref, low, mid, high = refs[6:]
    latent = updated_latent(r, latent_ref, (g0, g1, g2), part_ref, column_ref, refs[:6])
    decoded = jnp.maximum(mm(latent, dw1_ref[...]), 0.0)
    decoded = decoded.astype(BF16).astype(F32)
    acceleration = lax.dot_general(
        dw2_ref[...],
        decoded,
        (((1,), (1,)), ((), ())),
        precision=lax.Precision.HIGHEST,
        preferred_element_type=F32,
    )
    state_rows, particles = kin_ref.shape
    velocity = kin_ref[state_rows - 3 :, :] + acceleration
    state = jnp.concatenate([kin_ref[:3, :] + velocity, kin_ref[6:, :], velocity], axis=0)
    direction = dir_ref[...]
    staying = direction == 13
    stayed_ref[...] = jnp.where(staying, state, 0.0)
    dx, dy, dz = split_direction(direction)
    code = (dz * 9 + dx * 3 + dy) * MIG + slot_ref[...]
    code = jnp.where(staying, -1, code)
    picker = jnp.where(
        code == lax.broadcasted_iota(jnp.int32, (27 * MIG, particles), 0), 1.0, 0.0
    )
    outgoing = lax.dot_general(
        picker,
        state,
        (((1,), (1,)), ((), ())),
        precision=lax.Precision.HIGHEST,
        preferred_element_type=F32,
    )
    step = 9 * MIG
    by_parity([outgoing[i * step : (i + 1) * step] for i in range(3)], (low, mid, high))


def whole(shape):
    return pl.BlockSpec(shape, lambda i: (0,) * len(shape))


def call(body, args, specs, outs, name, flops=0, moved=0):
    return pl.pallas_call(
        body,
        grid=(1,),
        in_specs=[spec if spec is not None else whole(a.shape) for a, spec in zip(args, specs)],
        out_specs=[whole(s.shape) for s in outs],
        out_shape=outs,
        compiler_params=pltpu.CompilerParams(vmem_limit_bytes=VMEM_LIMIT),
        cost_estimate=pl.CostEstimate(flops=flops, bytes_accessed=moved, transcendentals=0),
        name=name,
    )(*args)


def fetching(body, count, *refs):
    sources, outs = refs[:count], refs[count : -count - 1]
    targets, sems = refs[-count - 1 : -1], refs[-1]
    copies = [
        pltpu.make_async_copy(source, target, sems.at[i])
        for i, (source, target) in enumerate(zip(sources, targets))
    ]
    for copy in copies:
        copy.start()
    for copy in copies:
        copy.wait()
    body(*targets, *outs)


def call_fetching(body, args, outs, name, flops=0, moved=0):
    return pl.pallas_call(
        functools.partial(fetching, body, len(args)),
        in_specs=[pl.BlockSpec(memory_space=pltpu.HBM)] * len(args),
        out_specs=[pl.BlockSpec(memory_space=pltpu.VMEM)] * len(outs),
        out_shape=outs,
        scratch_shapes=[pltpu.VMEM(a.shape, a.dtype) for a in args]
        + [pltpu.SemaphoreType.DMA((len(args),))],
        compiler_params=pltpu.CompilerParams(vmem_limit_bytes=FETCH_LIMIT),
        cost_estimate=pl.CostEstimate(flops=flops, bytes_accessed=moved, transcendentals=0),
        name=name,
    )(*args)


def shape(dims, dtype):
    return jax.ShapeDtypeStruct(dims, dtype)


def swapped(value, axis, first):
    pairs = []
    for low in range(first, lax.axis_size(axis) - 1, 2):
        pairs += [(low, low + 1), (low + 1, low)]
    return lax.ppermute(value, axis, pairs)


def moved_in_pairs(to_odd, mid, to_even, axis):
    even = lax.axis_index(axis) % 2 == 0
    odd_pairs = swapped(to_odd, axis, 1)
    even_pairs = swapped(to_even, axis, 0)
    from_below = jnp.where(even, odd_pairs, even_pairs)
    from_above = jnp.where(even, even_pairs, odd_pairs)
    return [from_below, mid, from_above]


def moved(low, mid, high, axis):
    return [shifted(high, axis, 1), mid, shifted(low, axis, -1)]


def exchanged(low, mid, high, rows):
    tail = low.shape[-1]
    parts = moved_in_pairs(low, mid, high, "gz")
    hold = parts[0]
    parts = [part.reshape(3, 3 * rows, tail) for part in parts]
    parts = moved(*(jnp.concatenate([part[x] for part in parts], axis=0) for x in range(3)), "gx")
    held = (hold, parts[0])
    parts = [part.reshape(3, 3, rows, tail) for part in parts]
    low, mid, high = (
        jnp.stack([part[:, y] for part in parts], axis=1).reshape(9 * rows, tail)
        for y in range(3)
    )
    return moved(low, mid, high, "gy"), held


def on_device(
    kinematics,
    pair_offsets,
    pair_index,
    neighbour_count,
    send_rows,
    migrate_dir,
    migrate_slot,
    enc_node_w1,
    enc_node_w2,
    enc_edge_w1,
    enc_edge_w2,
    edge_w1,
    edge_w2,
    node_w1,
    node_w2,
    edge_gain,
    node_gain,
    dec_w1,
    dec_w2,
):
    width = enc_node_w2.shape[1]
    slots, particles = pair_index.shape
    ghost_rows = send_rows.shape[1]
    rounds = edge_w1.shape[0]
    state_rows = kinematics.shape[0]
    rows = send_rows.T
    part = shape((9 * ghost_rows, width), BF16)
    latent, low, mid, high = call_fetching(
        node_kernel,
        (kinematics, enc_node_w1, enc_node_w2, rows),
        [shape((particles, width), BF16), part, part, part],
        "node_encoder",
    )
    edges, columns = call_fetching(
        edge_kernel,
        (
            pair_offsets,
            pair_index,
            neighbour_count.reshape(1, particles),
            enc_edge_w1,
            enc_edge_w2,
        ),
        [shape((slots, particles, width), BF16), shape((particles, 128), jnp.int32)],
        "edge_encoder",
        flops=2 * slots * particles * 256 * 384,
        moved=4 * slots * particles * width,
    )
    leaving = [migrate_dir.reshape(1, particles), migrate_slot.reshape(1, particles)]
    for r in range(rounds):
        ghosts, held = exchanged(low, mid, high, ghost_rows)

        def of_round(array):
            return pl.BlockSpec((1,) + array.shape[1:], lambda i: (r, 0, 0))

        held = (held[min(r, 1)],)
        (part_sum,) = call(
            local_kernel,
            (latent, edges, columns, edge_w1) + held,
            (None, None, None, of_round(edge_w1)) + (None,) * len(held),
            [shape((slots, particles, width), F32)],
            "local_pairs",
            flops=2 * slots * particles * 256 * 512,
            moved=8 * slots * particles * width,
        )
        weights = [edge_w1, edge_w2, node_w1, node_w2]
        args = [latent, *ghosts[::-1], part_sum, columns, *weights, edge_gain, node_gain]
        specs = [None] * 6 + [of_round(w) for w in weights] + [None, None]
        if r < rounds - 1:
            latent, low, mid, high = call(
                functools.partial(round_kernel, r),
                args + [rows],
                specs + [None],
                [shape((particles, width), BF16), part, part, part],
                "message_round",
            )
        else:
            out = shape((9 * MIG, state_rows), F32)
            stayed, low, mid, high = call(
                functools.partial(last_kernel, r),
                args + [kinematics, *leaving, dec_w1, dec_w2],
                specs + [None] * 5,
                [shape((state_rows, particles), F32), out, out, out],
                "last_round",
            )
    landed = jnp.stack(exchanged(low, mid, high, MIG)[0], axis=0)
    landed = landed.reshape(3, 3, 3, MIG, state_rows).transpose(4, 2, 0, 1, 3)
    return (stayed, landed.reshape(state_rows, 27 * MIG))


def solution(mesh):
    axes = ("gx", "gy", "gz")
    return jax.shard_map(
        on_device,
        mesh=mesh,
        in_specs=(
            P(None, axes),
            P(None, None, axes),
            P(None, axes),
            P(axes),
            P(None, axes),
            P(axes),
            P(axes),
        )
        + (P(),) * 12,
        out_specs=(P(None, axes), P(None, axes)),
        check_vma=False,
    )
```
